256 devices in a mesh: seg: 64 (over y_hi, x, z), fsdp: 4 (over y_lo, core).
Axes of the slice: x: 4, y: 4 (y_hi: 2, y_lo: 2; y = y_hi * 2 + y_lo), z: 8, core: 2. Of those that a mesh axis runs over, the one named last changes fastest.
Arguments:
- tokens: bfloat16 [4, 8192, 4096], P('fsdp', 'seg'), may hold values from -6 to 6
- w_kv: bfloat16 [4096, 4096], P('fsdp'), may hold values from -0.09375 to 0.09375
- q_state: bfloat16 [256, 2048], P('fsdp'), may hold values from -400 to 400
- decay: float32 [64, 2048], P('seg'), may hold values from 0 to 1
Outputs:
- states: bfloat16 [4, 64, 256, 2048], P('fsdp', 'seg')
The draws below stay inside these ranges and needn't reach their ends.
All inputs are finite; a program needn't handle non-finite values.
Results may differ from the reference program's by a relative error of at most 0.011.
Values may be sent and summed in bfloat16 or wider, within the bound.
No kernel may reach another device: no remote copies, remote signals or barrier semaphores. Data moves between devices by JAX's collectives and lax.ppermute only.
A program may use at most 320 MiB of HBM per device.

```python
import math
import jax
import jax.numpy as jnp
from jax import lax

D = 4096
HEADS = 16
HS = 128
S = 256
SEG_LEN = 128
HD = 2048
SEGMENT_COUNT = 64
BATCH = 4
LENGTH = 8192


def draw_q_state(key, part):
    key = jax.random.fold_in(key, 11)
    first = jax.random.fold_in(key, 0)
    values = jax.random.normal(first, (S, HEADS * HS), jnp.float32)
    return jnp.clip(values, -4.0, 4.0).astype(jnp.bfloat16)


def draw_decay(key, part):
    key = jax.random.fold_in(key, 23)
    key_vectors = jax.random.split(key, 6)
    width = HEADS * HS
    slow_share = 0.5
    slow = jax.random.uniform(key_vectors[0], (width,), jnp.float32) < slow_share
    slow_rate = math.log(10.0) / SEGMENT_COUNT * jax.random.uniform(key_vectors[1], (width,), jnp.float32, 0.2, 1.0)
    fast_rate = jax.random.uniform(key_vectors[2], (width,), jnp.float32, 0.5, 1.5)
    base_rate = jnp.where(slow, slow_rate, fast_rate)
    jitter = jax.random.uniform(key_vectors[3], (SEGMENT_COUNT, width), jnp.float32, 0.5, 1.5)
    gate_values = jnp.exp(-base_rate[None, :] * jitter)
    group_token_rows = jax.random.randint(key_vectors[4], (3,), 0, SEGMENT_COUNT)
    match_flags = jnp.any(jnp.arange(SEGMENT_COUNT)[:, None] == group_token_rows[None, :], axis=1)
    group_token_count = jax.random.uniform(key_vectors[5], (SEGMENT_COUNT, 1), jnp.float32, 0.5, 0.8)
    return gate_values * jnp.where(match_flags[:, None], group_token_count, 1.0)


def steps_of(stream_key, shape, pieces, smallest, largest):
    factor_of, own = 1.0, jax.random.fold_in(stream_key, 6)
    for axis_at, blocks in pieces:
        heights = jnp.exp(jax.random.uniform(jax.random.fold_in(own, axis_at), (blocks,), jnp.float32, smallest / len(pieces), largest / len(pieces)))
        factor_of = factor_of * jnp.repeat(heights, shape[axis_at] // blocks).reshape([-1 if axis == axis_at else 1 for axis in range(len(shape))])
    return factor_of


def centred(stream_key, dims, scale, limit, cuts=(), kind=jnp.bfloat16):
    loudness = steps_of(stream_key, dims, cuts, -0.22, 0.18) if cuts else 1.0
    entries = jax.random.normal(stream_key, dims, jnp.float32) * scale * loudness
    return jnp.minimum(jnp.maximum(entries, -limit), limit).astype(kind)


def setup_inputs(seed: int = 0) -> dict:
    arg_keys = jax.random.split(jax.random.key(seed), 5)
    return {
        "tokens": centred(arg_keys[0], (BATCH, LENGTH, D), 1.0, 6.0, ((0, 4), (1, 64))),
        "w_kv": centred(arg_keys[1], (D, 2 * HD), D ** -0.5, 0.09375, ((0, 4),)),
        "q_state": draw_q_state(jax.random.fold_in(arg_keys[4], 71), 0),
        "decay": draw_decay(jax.random.fold_in(arg_keys[4], 71), 0),
    }


def reference(tokens, w_kv, q_state, decay):
    score_scale = 1.0 / math.sqrt(HS)
    query = q_state.astype(jnp.float32).reshape(S, HEADS, HS)

    def one_sequence(sequence):

        def one_segment(carried, inputs):
            segment_rows, decay_row = inputs
            projected = jnp.dot(segment_rows, w_kv, preferred_element_type=jnp.float32)
            projected = projected.astype(jnp.bfloat16).astype(jnp.float32)
            key_heads = projected[:, :HEADS * HS].reshape(SEG_LEN, HEADS, HS)
            value_heads = projected[:, HEADS * HS:].reshape(SEG_LEN, HEADS, HS)
            scores = jnp.einsum('rhe,the->hrt', query, key_heads) * score_scale
            weights = jax.nn.softmax(scores, axis=-1).astype(jnp.bfloat16).astype(jnp.float32)
            update = jnp.einsum('hrt,the->rhe', weights, value_heads).reshape(S, HEADS * HS)
            state = decay_row[None, :] * carried + update
            return (state, state.astype(jnp.bfloat16))
        segment_blocks = sequence.reshape(SEGMENT_COUNT, SEG_LEN, D)
        _, all_states = lax.scan(one_segment, jnp.zeros((S, HEADS * HS), jnp.float32), (segment_blocks, decay))
        return all_states
    return lax.map(one_sequence, tokens)
```

```python
import functools
import math

import jax
import jax.numpy as jnp
from jax import lax
from jax.experimental import pallas as pl
from jax.experimental.pallas import tpu as pltpu
from jax.sharding import PartitionSpec as P

HEADS = 16
HS = 128
S = 256
SEG = 64
TOK = 128
D = 4096
HD = 2048
QUARTER = D // 4
HALF = HD // 2
BOTH = ("seg", "fsdp")
BF = jnp.bfloat16
F32 = jnp.float32


def flat(y, x, z, core):
    return (((y // 2) * 4 + x) * 8 + z) * 4 + (y % 2) * 2 + core


def moves(dy, dc):
    pairs = []
    for y in range(4):
        for x in range(4):
            for z in range(8):
                for core in range(2):
                    pairs.append((flat(y, x, z, core), flat((y + dy) % 4, x, z, (core + dc) % 2)))
    return pairs


UP, DOWN = moves(1, 0), moves(-1, 0)
UP_X, DOWN_X = moves(1, 1), moves(-1, 1)
SIB = moves(0, 1)


def send(value, pairs):
    return lax.ppermute(value, BOTH, pairs)


TILE = 512


def project_kernel(core_ref, *refs, splits):
    pieces = refs[: len(splits)]
    w_ref, sk_ref, sv_ref = refs[len(splits) : len(splits) + 3]
    outs = refs[len(splits) + 3 : -1]
    x_ref = refs[-1]
    step = pl.program_id(0)
    core = core_ref[0]

    @pl.when(step == 0)
    def _():
        at = 0
        for piece, rows in zip(pieces, splits):
            x_ref[at : at + rows, :] = piece[...]
            at += rows

    own = pl.ds(pl.multiple_of(core * QUARTER, QUARTER), QUARTER)
    other = pl.ds(pl.multiple_of((1 - core) * QUARTER, QUARTER), QUARTER)

    def emit(sib):
        total = jnp.dot(x_ref[:, own], w_ref[...], preferred_element_type=F32)
        total += jnp.dot(x_ref[:, other], sib[...], preferred_element_type=F32)
        at = 0
        for out in outs:
            rows = out.shape[0]
            out[...] = total[at : at + rows].astype(out.dtype)
            at += rows

    half = HALF // TILE

    @pl.when(step < half)
    def _():
        emit(sk_ref)

    @pl.when(step >= half)
    def _():
        emit(sv_ref)


def project(core, pieces, w, sib_k, sib_v, out_rows, dtype):
    half = HALF // TILE
    splits = [p.shape[0] for p in pieces]
    total = sum(splits)

    def w_map(j, core_ref):
        return (0, (j // half) * (HD // TILE) + core_ref[0] * half + j % half)

    return pl.pallas_call(
        functools.partial(project_kernel, splits=splits),
        grid_spec=pltpu.PrefetchScalarGridSpec(
            num_scalar_prefetch=1,
            grid=(2 * half,),
            in_specs=[pl.BlockSpec(p.shape, lambda j, c: (0, 0)) for p in pieces]
            + [
                pl.BlockSpec((QUARTER, TILE), w_map),
                pl.BlockSpec((QUARTER, TILE), lambda j, c: (0, jnp.minimum(j, half - 1))),
                pl.BlockSpec((QUARTER, TILE), lambda j, c: (0, jnp.maximum(j - half, 0))),
            ],
            out_specs=[pl.BlockSpec((rows, TILE), lambda j, c: (0, j)) for rows in out_rows],
            scratch_shapes=[pltpu.VMEM((total, 2 * QUARTER), BF)],
        ),
        out_shape=[jax.ShapeDtypeStruct((rows, HD), dtype) for rows in out_rows],
        compiler_params=pltpu.CompilerParams(vmem_limit_bytes=40 << 20),
        cost_estimate=pl.CostEstimate(
            flops=2 * total * 2 * QUARTER * HD, bytes_accessed=2 * 2 * QUARTER * HD + total * HD * 8, transcendentals=0
        ),
    )(core, *pieces, w, sib_k, sib_v)


def one_head(q, k, v):
    scores = lax.dot_general(q, k, (((1,), (1,)), ((), ())), preferred_element_type=F32) * (1.0 / math.sqrt(HS))
    scores = jnp.exp(scores - jnp.max(scores, axis=1, keepdims=True))
    weights = (scores / jnp.sum(scores, axis=1, keepdims=True)).astype(BF)
    return jnp.dot(weights, v, preferred_element_type=F32).astype(BF)


def attend_kernel(core_ref, *refs):
    q_own, q_other, out_ref = refs[-3:]
    core = core_ref[0]
    j = pl.program_id(0)
    for at, q_ref, half in ((0, q_own, core), (6, q_other, 1 - core)):
        ak, av, pk, pv, mk, mv = refs[at : at + 6]
        k = (ak[...] + jnp.concatenate([pk[...], mk[...]], axis=0).astype(F32)).astype(BF)
        v = (av[...] + jnp.concatenate([pv[...], mv[...]], axis=0).astype(F32)).astype(BF)
        out_ref[half * (HEADS // 2) + j] = one_head(q_ref[...], k, v)


def attend(core, own, other, q):
    heads = HEADS // 2
    in_specs, args = [], []
    for local, up, down in (own, other):
        for part in (local, up, down):
            for shift in (0, heads):
                in_specs.append(pl.BlockSpec((part.shape[0], HS), lambda j, c, shift=shift: (0, j + shift)))
                args.append(part)
    in_specs.append(pl.BlockSpec((S, HS), lambda j, c: (0, c[0] * heads + j)))
    in_specs.append(pl.BlockSpec((S, HS), lambda j, c: (0, (1 - c[0]) * heads + j)))
    return pl.pallas_call(
        attend_kernel,
        grid_spec=pltpu.PrefetchScalarGridSpec(
            num_scalar_prefetch=1,
            grid=(heads,),
            in_specs=in_specs,
            out_specs=pl.BlockSpec((HEADS, S, HS), lambda j, c: (0, 0, 0)),
        ),
        out_shape=jax.ShapeDtypeStruct((HEADS, S, HS), BF),
        compiler_params=pltpu.CompilerParams(vmem_limit_bytes=32 << 20),
        cost_estimate=pl.CostEstimate(flops=4 * HEADS * S * TOK * HS, bytes_accessed=5 << 20, transcendentals=HEADS * S * TOK),
    )(core, *args, q, q)


SCAN_STEP = 16


def scan_kernel(decay_ref, update_ref, out_ref, carry_ref):
    @pl.when(pl.program_id(0) == 0)
    def _():
        carry_ref[...] = jnp.zeros_like(carry_ref)

    carry = carry_ref[...]
    for i in range(SCAN_STEP):
        carry = decay_ref[i] * carry + update_ref[i].astype(F32)
        out_ref[i] = carry.astype(BF)
    carry_ref[...] = carry


def scan(decay, update):
    rows = update.shape[1]
    return pl.pallas_call(
        scan_kernel,
        grid=(SEG // SCAN_STEP,),
        in_specs=[
            pl.BlockSpec((SCAN_STEP, 1, HS), lambda i: (i, 0, 0)),
            pl.BlockSpec((SCAN_STEP, rows, HS), lambda i: (i, 0, 0)),
        ],
        out_specs=pl.BlockSpec((SCAN_STEP, rows, HS), lambda i: (i, 0, 0)),
        out_shape=jax.ShapeDtypeStruct(update.shape, BF),
        scratch_shapes=[pltpu.VMEM((rows, HS), F32)],
        cost_estimate=pl.CostEstimate(flops=2 * update.size, bytes_accessed=4 * update.size, transcendentals=0),
    )(decay, update)


def gather_queries(q, y_lo, core):
    rows = q.shape[0] // 2
    far = jnp.concatenate([send(q[:rows], UP), send(q[rows:], DOWN)], axis=0)
    pair = jnp.concatenate([q, far], axis=0)
    sib = send(pair, SIB)
    near0 = jnp.where(core == 0, pair, sib)
    near1 = jnp.where(core == 0, sib, pair)
    n = q.shape[0]
    mine = jnp.concatenate([near0[:n], near1[:n]], axis=0)
    theirs = jnp.concatenate([near0[n:], near1[n:]], axis=0)
    return jnp.concatenate([jnp.where(y_lo == 0, mine, theirs), jnp.where(y_lo == 0, theirs, mine)], axis=0)


def body(tokens, w_kv, q_state, decay):
    own_tokens = tokens[0]
    place = lax.axis_index("fsdp")
    y_lo, core = place // 2, place % 2
    core_arg = core.astype(jnp.int32).reshape(1)
    away = lax.dynamic_slice_in_dim(own_tokens, (1 - y_lo) * 2 * QUARTER, 2 * QUARTER, axis=1)
    home = lax.dynamic_slice_in_dim(own_tokens, y_lo * 2 * QUARTER, 2 * QUARTER, axis=1)
    lower = send(away[: TOK // 2], UP)
    upper = send(away[TOK // 2 :], DOWN)
    sib_k = send(lax.dynamic_slice_in_dim(w_kv, (1 - core) * HALF, HALF, axis=1), SIB)
    sib_v = send(lax.dynamic_slice_in_dim(w_kv, HD + (1 - core) * HALF, HALF, axis=1), SIB)
    sib_home = send(home, SIB)
    gate = jnp.repeat(decay[0].reshape(HEADS, 1, HS), S // 64, axis=0)
    gate = lax.all_to_all(gate, "seg", 0, 0, tiled=True)
    query = gather_queries(q_state, y_lo, core)
    lower_sib, upper_sib = send(lower, SIB), send(upper, SIB)

    half_rows = TOK // 2
    far = project(core_arg, [lower, lower_sib, upper, upper_sib], w_kv, sib_k, sib_v, [half_rows] * 4, BF)
    own_up, own_down = send(far[0], DOWN), send(far[2], UP)
    other_up, other_down = send(far[1], DOWN_X), send(far[3], UP_X)
    near, near_sib = project(core_arg, [home, sib_home], w_kv, sib_k, sib_v, [TOK] * 2, F32)
    near_other = send(near_sib, SIB)
    update = attend(core_arg, (near, own_up, own_down), (near_other, other_up, other_down), query)
    update = lax.all_to_all(update.reshape(SEG, S // 4, HS), "seg", 0, 0, tiled=True)
    states = scan(gate, update)
    states = lax.all_to_all(states, "seg", 0, 0, tiled=True)
    states = states.reshape(HEADS, S, HS).transpose(1, 0, 2).reshape(S, HD)
    return states[None, None]


def solution(mesh):
    return jax.shard_map(
        body,
        mesh=mesh,
        in_specs=(P("fsdp", "seg", None), P("fsdp", None), P("fsdp", None), P("seg", None)),
        out_specs=P("fsdp", "seg", None, None),
        check_vma=False,
    )
```

```python
import functools
import math

import jax
import jax.numpy as jnp
from jax import lax
from jax.experimental import pallas as pl
from jax.experimental.pallas import tpu as pltpu
from jax.sharding import PartitionSpec as P

HEADS = 16
HS = 128
S = 256
SEG = 64
TOK = 128
D = 4096
HD = 2048
QUARTER = D // 4
HALF = HD // 2
BOTH = ("seg", "fsdp")
BF = jnp.bfloat16
F32 = jnp.float32


def flat(y, x, z, core):
    return (((y // 2) * 4 + x) * 8 + z) * 4 + (y % 2) * 2 + core


def moves(dy, dc):
    pairs = []
    for y in range(4):
        for x in range(4):
            for z in range(8):
                for core in range(2):
                    pairs.append((flat(y, x, z, core), flat((y + dy) % 4, x, z, (core + dc) % 2)))
    return pairs


UP, DOWN, SIB = moves(1, 0), moves(-1, 0), moves(0, 1)


def send(value, pairs):
    return lax.ppermute(value, BOTH, pairs)


TILE = 256
WIDE = 2 * QUARTER
PART = TOK // 2
Q_ROWS = S // 4
BLOCK = S // 4
GATE_ROWS = 8

ANY = pl.BlockSpec(memory_space=pl.ANY)
HBM = pl.BlockSpec(memory_space=pltpu.HBM)
VMEM = pl.BlockSpec(memory_space=pltpu.VMEM)


def here(value):
    return pltpu.with_memory_space_constraint(value, pltpu.VMEM)


def far_away(value):
    return pltpu.with_memory_space_constraint(value, pltpu.HBM)


def position():
    fsdp = lax.axis_index("fsdp")
    return fsdp % 2, fsdp // 2


def half_of(which, size):
    return pl.ds(pl.multiple_of(which * size, size), size)


def run_copies(pairs, sems):
    todo = [pltpu.make_async_copy(a, b, sems.at[i]) for i, (a, b) in enumerate(pairs)]
    for c in todo:
        c.start()
    for c in todo:
        c.wait()


PARAMS = pltpu.CompilerParams(vmem_limit_bytes=8 << 20)


def cost(flops, nbytes, exps=0):
    return pl.CostEstimate(flops=flops, bytes_accessed=nbytes, transcendentals=exps)


CUT_ROWS = 256


def cut_pairs(w_ref, out_ref, half):
    pairs = []
    for v in range(2):
        cols = pl.ds(pl.multiple_of(v * HD + half * HALF, HALF), HALF)
        for r in range(0, QUARTER, CUT_ROWS):
            rows = slice(r, r + CUT_ROWS)
            pairs.append((w_ref.at[rows, cols], out_ref.at[rows, v * HALF : (v + 1) * HALF]))
    return pairs


CUT_COPIES = 2 * QUARTER // CUT_ROWS


def sort_kernel(tokens_ref, q_ref, w_ref, up_ref, down_ref, sib_ref, w_out, sems):
    core, y_lo = position()
    home, away = half_of(y_lo, WIDE), half_of(1 - y_lo, WIDE)
    run_copies(
        [
            (tokens_ref.at[:PART, away], up_ref),
            (tokens_ref.at[PART:, away], down_ref),
            (tokens_ref.at[:PART, home], sib_ref.at[:PART]),
            (tokens_ref.at[PART:, home], sib_ref.at[PART:TOK]),
            (q_ref, sib_ref.at[TOK:]),
        ]
        + cut_pairs(w_ref, w_out, 1 - core),
        sems,
    )


def sort_inputs(tokens, q, w):
    shapes = [(PART, WIDE), (PART, WIDE), (TOK + Q_ROWS, WIDE), (QUARTER, HD)]
    return pl.pallas_call(
        sort_kernel,
        in_specs=[HBM] * 3,
        out_specs=[VMEM] * 4,
        out_shape=[pltpu.VMEM(shape, BF) for shape in shapes],
        scratch_shapes=[pltpu.SemaphoreType.DMA((5 + CUT_COPIES,))],
        compiler_params=PARAMS,
        cost_estimate=cost(0, 12 << 20),
    )(far_away(tokens), far_away(q), far_away(w))


def project_kernel(*refs, rows, extra):
    n = len(rows)
    pieces, w_ref, sib_ref, outs = refs[:n], refs[n], refs[n + 1], refs[n + 2 + extra : n + 4 + extra]
    x_ref, own_w, own_sems, x_sems = refs[n + 4 + extra :]
    core, _ = position()
    pairs, start = [], 0
    for piece, count in zip(pieces, rows):
        pairs.append((piece.at[:count], x_ref.at[start : start + count]))
        start += count
    half = start // 2
    for ref, out in zip(refs[n + 2 : n + 2 + extra], outs):
        for i in range(2):
            block = slice(TOK + i * Q_ROWS // 2, TOK + (i + 1) * Q_ROWS // 2)
            pairs.append((ref.at[block, half_of(core, HALF)], out.at[half:, i * HALF : (i + 1) * HALF]))
    x_copies = [pltpu.make_async_copy(a, b, x_sems.at[i]) for i, (a, b) in enumerate(pairs)]
    own_copies = [pltpu.make_async_copy(a, b, own_sems.at[i]) for i, (a, b) in enumerate(cut_pairs(w_ref, own_w, core))]
    for copy in x_copies[:n]:
        copy.start()
    for copy in own_copies:
        copy.start()
    for copy in x_copies[n:]:
        copy.start()
    for copy in x_copies[:n]:
        copy.wait()
    x_own, x_other = x_ref[:, half_of(core, QUARTER)], x_ref[:, half_of(1 - core, QUARTER)]
    for v in range(2):
        cols = slice(v * HALF, (v + 1) * HALF)
        mine = slice(v * CUT_COPIES // 2, (v + 1) * CUT_COPIES // 2)
        total = jnp.dot(x_other, sib_ref[:, cols], preferred_element_type=F32)
        for copy in own_copies[mine]:
            copy.wait()
        total += jnp.dot(x_own, own_w[:, cols], preferred_element_type=F32)
        for i, out in enumerate(outs):
            out[:half, cols] = total[i * half : (i + 1) * half].astype(out.dtype)
    for copy in x_copies[n:]:
        copy.wait()


def project(pieces, w, sib_w, dtype, queries=()):
    rows = [count for _, count in pieces]
    total = sum(rows)
    height = total // 2 + (Q_ROWS // 2 if queries else 0)
    args = [p for p, _ in pieces] + [far_away(w), sib_w, *queries]
    return pl.pallas_call(
        functools.partial(project_kernel, rows=rows, extra=len(queries)),
        in_specs=[ANY] * len(pieces) + [HBM, VMEM] + [ANY] * len(queries),
        out_specs=[VMEM] * 2,
        out_shape=[pltpu.VMEM((height, HD), dtype) for _ in range(2)],
        scratch_shapes=[
            pltpu.VMEM((total, WIDE), BF),
            pltpu.VMEM((QUARTER, HD), BF),
            pltpu.SemaphoreType.DMA((CUT_COPIES,)),
            pltpu.SemaphoreType.DMA((len(pieces) + 4,)),
        ],
        compiler_params=pltpu.CompilerParams(vmem_limit_bytes=14 << 20),
        cost_estimate=cost(2 * total * WIDE * HD, 4 * WIDE * HD),
    )(*args)


def one_head(q, k, v):
    scores = lax.dot_general(q, k, (((1,), (1,)), ((), ())), preferred_element_type=F32) * (1.0 / math.sqrt(HS))
    scores = jnp.exp(scores - jnp.max(scores, axis=1, keepdims=True))
    weights = (scores / jnp.sum(scores, axis=1, keepdims=True)).astype(BF)
    return jnp.dot(weights, v, preferred_element_type=F32).astype(BF)


def attend_kernel(near0, near1, low_ref, up_ref, own_ref, sib_ref, gate_ref, out_ref):
    core, y_lo = position()
    place = y_lo * 2 + core
    for head in range(HEADS // 2):
        q_cols = pl.ds(pl.multiple_of(core * HALF + head * HS, HS), HS)
        k_cols, v_cols = slice(head * HS, (head + 1) * HS), slice(HALF + head * HS, HALF + (head + 1) * HS)
        parts = [own_ref[TOK:, q_cols], sib_ref[TOK:, q_cols]]
        for ref in (up_ref, low_ref):
            parts += [ref[TOK:, k_cols], ref[TOK:, v_cols]]
        q = jnp.concatenate(parts, axis=0)
        gate = gate_ref[:, q_cols]
        terms = []
        for _ in range(3):
            terms.append(gate.astype(BF))
            gate = gate - terms[-1].astype(F32)
        gate = jnp.concatenate([t.astype(F32) for t in terms] + [jnp.zeros((GATE_ROWS - 3, HS), F32)], axis=0).astype(BF)
        for batch, near in enumerate((near0, near1)):
            rows = slice(batch * PART, (batch + 1) * PART)

            def total(cols):
                far = jnp.concatenate([low_ref[rows, cols], up_ref[rows, cols]], axis=0)
                return (near[:, cols] + far.astype(F32)).astype(BF)

            update = one_head(q, total(k_cols), total(v_cols))
            for i in range(S // BLOCK):
                at = (batch * (HEADS // 2) + head) * (S // BLOCK) + (place ^ i)
                out_ref[at, :BLOCK] = update[i * BLOCK : (i + 1) * BLOCK]
                out_ref[at, BLOCK:] = gate


def attend(near, far, queries, gate):
    args = [*near, *far, *queries, gate]
    return pl.pallas_call(
        attend_kernel,
        in_specs=[VMEM] * len(args),
        out_specs=VMEM,
        out_shape=pltpu.VMEM((SEG, BLOCK + GATE_ROWS, HS), BF),
        compiler_params=PARAMS,
        cost_estimate=cost(8 * HEADS // 2 * S * TOK * HS, 6 << 20, HEADS * S * TOK),
    )(*args)


def scan_kernel(update_ref, out_ref):
    def step(i, carry):
        terms = update_ref[i, BLOCK:].astype(F32)
        gate = terms[0:1] + terms[1:2] + terms[2:3]
        carry = gate * carry + update_ref[i, :BLOCK].astype(F32)
        out_ref[i] = carry.astype(BF)
        return carry

    lax.fori_loop(0, SEG, step, jnp.zeros((BLOCK, HS), F32), unroll=8)


def scan(update):
    return pl.pallas_call(
        scan_kernel,
        in_specs=[VMEM],
        out_specs=VMEM,
        out_shape=pltpu.VMEM((SEG, BLOCK, HS), BF),
        compiler_params=PARAMS,
        cost_estimate=cost(2 * SEG * BLOCK * HS, 4 * SEG * BLOCK * HS),
    )(here(update))


def place_kernel(own_ref, other_ref, out_ref, sems):
    core, _ = position()
    pairs = []
    for batch, (ref, half) in enumerate(((own_ref, core), (other_ref, 1 - core))):
        for j in range(HEADS // 2):
            cols = pl.ds(pl.multiple_of(half * HALF + j * HS, HS), HS)
            pairs.append((ref.at[batch, j], out_ref.at[:, cols]))
    run_copies(pairs, sems)


def place(own, other):
    return pl.pallas_call(
        place_kernel,
        in_specs=[VMEM, VMEM],
        out_specs=ANY,
        out_shape=jax.ShapeDtypeStruct((S, HD), BF),
        scratch_shapes=[pltpu.SemaphoreType.DMA((HEADS,))],
        compiler_params=PARAMS,
        cost_estimate=cost(0, 4 * S * HD),
    )(here(own), here(other))


def spread(value):
    return lax.all_to_all(value, "seg", 0, 0, tiled=True)


def body(tokens, w_kv, q_state, decay):
    to_up, to_down, to_sib, to_sib_w = sort_inputs(tokens[0], q_state, w_kv)
    low, up, sib, sib_w = send(to_up, UP), send(to_down, DOWN), send(to_sib, SIB), send(to_sib_w, SIB)
    low_sib, up_sib = send(low, SIB), send(up, SIB)

    away = [(part, PART) for part in (low, low_sib, up, up_sib)]
    lower, upper = project(away, w_kv, sib_w, BF, (sib, to_sib))
    far = send(lower, DOWN), send(upper, UP)
    near = project([(to_sib, TOK), (sib, TOK)], w_kv, sib_w, F32)
    states = spread(scan(spread(attend(near, far, (to_sib, sib), decay))))
    other = send(states, SIB)
    shape = (2, HEADS // 2, S, HS)
    return place(states.reshape(shape), other.reshape(shape))[None, None]


def solution(mesh):
    return jax.shard_map(
        body,
        mesh=mesh,
        in_specs=(P("fsdp", "seg", None), P("fsdp", None), P("fsdp", None), P("seg", None)),
        out_specs=P("fsdp", "seg", None, None),
        check_vma=False,
    )
```

```python
import functools
import math

import jax
import jax.numpy as jnp
from jax import lax
from jax.experimental import pallas as pl
from jax.experimental.pallas import tpu as pltpu
from jax.sharding import PartitionSpec as P

HEADS = 16
HS = 128
S = 256
SEG = 64
TOK = 128
D = 4096
HD = 2048
QUARTER = D // 4
HALF = HD // 2
BOTH = ("seg", "fsdp")
BF = jnp.bfloat16
F32 = jnp.float32


def flat(y, x, z, core):
    return (((y // 2) * 4 + x) * 8 + z) * 4 + (y % 2) * 2 + core


def moves(dy, dc):
    pairs = []
    for y in range(4):
        for x in range(4):
            for z in range(8):
                for core in range(2):
                    pairs.append((flat(y, x, z, core), flat((y + dy) % 4, x, z, (core + dc) % 2)))
    return pairs


UP, DOWN, SIB, DOWN_X = moves(1, 0), moves(-1, 0), moves(0, 1), moves(-1, 1)


def send(value, pairs):
    return lax.ppermute(value, BOTH, pairs)


TILE = 256
WIDE = 2 * QUARTER
PART = TOK // 2
Q_ROWS = S // 4
BLOCK = S // 4
GATE_ROWS = 8

ANY = pl.BlockSpec(memory_space=pl.ANY)
HBM = pl.BlockSpec(memory_space=pltpu.HBM)
VMEM = pl.BlockSpec(memory_space=pltpu.VMEM)


def here(value):
    return pltpu.with_memory_space_constraint(value, pltpu.VMEM)


def far_away(value):
    return pltpu.with_memory_space_constraint(value, pltpu.HBM)


def position():
    fsdp = lax.axis_index("fsdp")
    return fsdp % 2, fsdp // 2


def half_of(which, size):
    return pl.ds(pl.multiple_of(which * size, size), size)


def run_copies(pairs, sems):
    todo = [pltpu.make_async_copy(a, b, sems.at[i]) for i, (a, b) in enumerate(pairs)]
    for c in todo:
        c.start()
    for c in todo:
        c.wait()


PARAMS = pltpu.CompilerParams(vmem_limit_bytes=8 << 20)


def cost(flops, nbytes, exps=0):
    return pl.CostEstimate(flops=flops, bytes_accessed=nbytes, transcendentals=exps)


CUT_ROWS = 256


def cut_pairs(w_ref, out_ref, half, values):
    cols = pl.ds(pl.multiple_of(values * HD + half * HALF, HALF), HALF)
    pairs = []
    for r in range(0, QUARTER, CUT_ROWS):
        rows = slice(r, r + CUT_ROWS)
        pairs.append((w_ref.at[rows, cols], out_ref.at[rows]))
    return pairs


CUT_COPIES = QUARTER // CUT_ROWS


def sort_kernel(tokens_ref, q_ref, w_ref, up_ref, down_ref, sib_ref, q_up_ref, q_down_ref, keys_out, values_out, sems):
    core, y_lo = position()
    home, away = half_of(y_lo, WIDE), half_of(1 - y_lo, WIDE)
    run_copies(
        [
            (tokens_ref.at[:PART, away], up_ref),
            (tokens_ref.at[PART:, away], down_ref),
            (tokens_ref.at[:PART, home], sib_ref.at[:PART]),
            (tokens_ref.at[PART:, home], sib_ref.at[PART:TOK]),
            (q_ref, sib_ref.at[TOK:]),
            (q_ref.at[:, half_of(core, HALF)], q_up_ref),
            (q_ref.at[:, half_of(1 - core, HALF)], q_down_ref),
        ]
        + cut_pairs(w_ref, keys_out, 1 - core, 0)
        + cut_pairs(w_ref, values_out, 1 - core, 1),
        sems,
    )


def sort_inputs(tokens, q, w):
    shapes = [(PART, WIDE), (PART, WIDE), (TOK + Q_ROWS, WIDE), (Q_ROWS, HALF), (Q_ROWS, HALF), (QUARTER, HALF), (QUARTER, HALF)]
    return pl.pallas_call(
        sort_kernel,
        in_specs=[HBM] * 3,
        out_specs=[VMEM] * 7,
        out_shape=[pltpu.VMEM(shape, BF) for shape in shapes],
        scratch_shapes=[pltpu.SemaphoreType.DMA((7 + 2 * CUT_COPIES,))],
        compiler_params=PARAMS,
        cost_estimate=cost(0, 12 << 20),
    )(far_away(tokens), far_away(q), far_away(w))


def project_kernel(*refs, rows, extra, parts):
    n = len(rows)
    pieces, w_ref, sib_refs = refs[:n], refs[n], refs[n + 1 : n + 1 + len(parts)]
    refs = refs[n + 1 + len(parts) :]
    outs, (x_ref, own_w, own_sems, x_sems) = refs[extra : extra + 2], refs[extra + 2 :]
    core, _ = position()
    pairs, start = [], 0
    for piece, count in zip(pieces, rows):
        pairs.append((piece.at[:count], x_ref.at[start : start + count]))
        start += count
    half = start // 2
    x_copies = [pltpu.make_async_copy(a, b, x_sems.at[i]) for i, (a, b) in enumerate(pairs)]
    own_copies = []
    for i, values in enumerate(parts):
        for k, (a, b) in enumerate(cut_pairs(w_ref, own_w.at[i], core, values)):
            own_copies.append(pltpu.make_async_copy(a, b, own_sems.at[i * CUT_COPIES + k]))
    for copy in x_copies + own_copies:
        copy.start()
    for copy in x_copies:
        copy.wait()
    x_own, x_other = x_ref[:, half_of(core, QUARTER)], x_ref[:, half_of(1 - core, QUARTER)]
    for i in range(len(parts)):
        cols = slice(i * HALF, (i + 1) * HALF)
        total = jnp.dot(x_other, sib_refs[i][...], preferred_element_type=F32)
        for copy in own_copies[i * CUT_COPIES : (i + 1) * CUT_COPIES]:
            copy.wait()
        total += jnp.dot(x_own, own_w[i], preferred_element_type=F32)
        for k, out in enumerate(outs):
            out[:, cols] = total[k * half : (k + 1) * half].astype(out.dtype)


def project(pieces, w, sib_w, parts, dtype, after=()):
    rows = [count for _, count in pieces]
    total = sum(rows)
    wide = len(parts) * HALF
    args = [p for p, _ in pieces] + [far_away(w), *[sib_w[i] for i in parts], *after]
    return pl.pallas_call(
        functools.partial(project_kernel, rows=rows, extra=len(after), parts=parts),
        in_specs=[ANY] * len(pieces) + [HBM] + [VMEM] * len(parts) + [ANY] * len(after),
        out_specs=[VMEM] * 2,
        out_shape=[pltpu.VMEM((total // 2, wide), dtype) for _ in range(2)],
        scratch_shapes=[
            pltpu.VMEM((total, WIDE), BF),
            pltpu.VMEM((len(parts), QUARTER, HALF), BF),
            pltpu.SemaphoreType.DMA((len(parts) * CUT_COPIES,)),
            pltpu.SemaphoreType.DMA((len(pieces),)),
        ],
        compiler_params=pltpu.CompilerParams(vmem_limit_bytes=14 << 20),
        cost_estimate=cost(2 * total * WIDE * wide, 4 * WIDE * wide),
    )(*args)


def one_head(q, k, v):
    scores = lax.dot_general(q, k, (((1,), (1,)), ((), ())), preferred_element_type=F32) * (1.0 / math.sqrt(HS))
    scores = jnp.exp(scores - jnp.max(scores, axis=1, keepdims=True))
    weights = (scores / jnp.sum(scores, axis=1, keepdims=True)).astype(BF)
    return jnp.dot(weights, v, preferred_element_type=F32).astype(BF)


def attend_kernel(near0, near1, low_k, up_k, low_v, up_v, own_ref, sib_ref, q_up, q_down, gate_ref, out_ref):
    core, y_lo = position()
    place = y_lo * 2 + core
    for head in range(HEADS // 2):
        cols = slice(head * HS, (head + 1) * HS)
        near_v = slice(HALF + head * HS, HALF + (head + 1) * HS)
        global_cols = pl.ds(pl.multiple_of(core * HALF + head * HS, HS), HS)
        q = jnp.concatenate(
            [own_ref[TOK:, global_cols], sib_ref[TOK:, global_cols], q_up[:, cols], q_down[:, cols]], axis=0
        )
        gate = gate_ref[:, global_cols]
        terms = []
        for _ in range(3):
            terms.append(gate.astype(BF))
            gate = gate - terms[-1].astype(F32)
        gate = jnp.concatenate([t.astype(F32) for t in terms] + [jnp.zeros((GATE_ROWS - 3, HS), F32)], axis=0).astype(BF)
        for batch, near in enumerate((near0, near1)):
            rows = slice(batch * PART, (batch + 1) * PART)
            k = near[:, cols] + jnp.concatenate([low_k[rows, cols], up_k[rows, cols]], axis=0).astype(F32)
            v = near[:, near_v] + jnp.concatenate([low_v[rows, cols], up_v[rows, cols]], axis=0).astype(F32)
            update = one_head(q, k.astype(BF), v.astype(BF))
            for i in range(S // BLOCK):
                at = (batch * (HEADS // 2) + head) * (S // BLOCK) + (place ^ i)
                out_ref[at, :BLOCK] = update[i * BLOCK : (i + 1) * BLOCK]
                out_ref[at, BLOCK:] = gate


def attend(near, far, queries, gate):
    args = [*near, *far, *queries, gate]
    return pl.pallas_call(
        attend_kernel,
        in_specs=[VMEM] * len(args),
        out_specs=VMEM,
        out_shape=pltpu.VMEM((SEG, BLOCK + GATE_ROWS, HS), BF),
        compiler_params=PARAMS,
        cost_estimate=cost(8 * HEADS // 2 * S * TOK * HS, 6 << 20, HEADS * S * TOK),
    )(*args)


def scan_kernel(update_ref, out_ref):
    def step(i, carry):
        terms = update_ref[i, BLOCK:].astype(F32)
        gate = terms[0:1] + terms[1:2] + terms[2:3]
        carry = gate * carry + update_ref[i, :BLOCK].astype(F32)
        out_ref[i] = carry.astype(BF)
        return carry

    lax.fori_loop(0, SEG, step, jnp.zeros((BLOCK, HS), F32), unroll=8)


def scan(update):
    return pl.pallas_call(
        scan_kernel,
        in_specs=[VMEM],
        out_specs=VMEM,
        out_shape=pltpu.VMEM((SEG, BLOCK, HS), BF),
        compiler_params=PARAMS,
        cost_estimate=cost(2 * SEG * BLOCK * HS, 4 * SEG * BLOCK * HS),
    )(here(update))


def place_kernel(own_ref, other_ref, out_ref, sems):
    core, _ = position()
    pairs = []
    for batch, (ref, half) in enumerate(((own_ref, core), (other_ref, 1 - core))):
        for j in range(HEADS // 2):
            cols = pl.ds(pl.multiple_of(half * HALF + j * HS, HS), HS)
            pairs.append((ref.at[batch, j], out_ref.at[:, cols]))
    run_copies(pairs, sems)


def place(own, other):
    return pl.pallas_call(
        place_kernel,
        in_specs=[VMEM, VMEM],
        out_specs=ANY,
        out_shape=jax.ShapeDtypeStruct((S, HD), BF),
        scratch_shapes=[pltpu.SemaphoreType.DMA((HEADS,))],
        compiler_params=PARAMS,
        cost_estimate=cost(0, 4 * S * HD),
    )(here(own), here(other))


def spread(value):
    return lax.all_to_all(value, "seg", 0, 0, tiled=True)


def body(tokens, w_kv, q_state, decay):
    to_up, to_down, to_sib, q_up, q_down, to_sib_k, to_sib_v = sort_inputs(tokens[0], q_state, w_kv)
    low, up, sib = send(to_up, UP), send(to_down, DOWN), send(to_sib, SIB)
    sib_w = send(to_sib_k, SIB), send(to_sib_v, SIB)
    q_far = send(q_up, UP), send(q_down, DOWN_X)
    low_sib, up_sib = send(low, SIB), send(up, SIB)

    away = [(part, PART) for part in (low, low_sib, up, up_sib)]
    lower, upper = project(away, w_kv, sib_w, (0,), BF)
    far_k = send(lower, DOWN), send(upper, UP)
    lower, upper = project(away, w_kv, sib_w, (1,), BF)
    far_v = send(lower, DOWN), send(upper, UP)
    near = project([(to_sib, TOK), (sib, TOK)], w_kv, sib_w, (0, 1), F32, q_far)
    states = spread(scan(spread(attend(near, far_k + far_v, (to_sib, sib) + q_far, decay))))
    other = send(states, SIB)
    shape = (2, HEADS // 2, S, HS)
    return place(states.reshape(shape), other.reshape(shape))[None, None]


def solution(mesh):
    return jax.shard_map(
        body,
        mesh=mesh,
        in_specs=(P("fsdp", "seg", None), P("fsdp", None), P("fsdp", None), P("seg", None)),
        out_specs=P("fsdp", "seg", None, None),
        check_vma=False,
    )
```

```python
import functools
import math

import jax
import jax.numpy as jnp
from jax import lax
from jax.experimental import pallas as pl
from jax.experimental.pallas import tpu as pltpu
from jax.sharding import PartitionSpec as P

HEADS = 16
HS = 128
S = 256
SEG = 64
TOK = 128
D = 4096
HD = 2048
QUARTER = D // 4
HALF = HD // 2
BOTH = ("seg", "fsdp")
BF = jnp.bfloat16
F32 = jnp.float32


def flat(y, x, z, core):
    return (((y // 2) * 4 + x) * 8 + z) * 4 + (y % 2) * 2 + core


def moves(steps, dc=0):
    pairs = []
    for y in range(4):
        for x in range(4):
            for z in range(8):
                for core in range(2):
                    pairs.append((flat(y, x, z, core), flat((y + steps[core]) % 4, x, z, (core + dc) % 2)))
    return pairs


OUT, BACK, SIB = moves((1, -1)), moves((-1, 1)), moves((0, 0), 1)


def send(value, pairs):
    return lax.ppermute(value, BOTH, pairs)


TILE = 256
WIDE = 2 * QUARTER
Q_ROWS = S // 4
BLOCK = S // 4
GATE_ROWS = 8

ANY = pl.BlockSpec(memory_space=pl.ANY)
HBM = pl.BlockSpec(memory_space=pltpu.HBM)
VMEM = pl.BlockSpec(memory_space=pltpu.VMEM)


def here(value):
    return pltpu.with_memory_space_constraint(value, pltpu.VMEM)


def far_away(value):
    return pltpu.with_memory_space_constraint(value, pltpu.HBM)


def position():
    fsdp = lax.axis_index("fsdp")
    return fsdp % 2, fsdp // 2


def half_of(which, size):
    return pl.ds(pl.multiple_of(which * size, size), size)


def run_copies(pairs, sems):
    todo = [pltpu.make_async_copy(a, b, sems.at[i]) for i, (a, b) in enumerate(pairs)]
    for c in todo:
        c.start()
    for c in todo:
        c.wait()


PARAMS = pltpu.CompilerParams(vmem_limit_bytes=8 << 20)


def cost(flops, nbytes, exps=0):
    return pl.CostEstimate(flops=flops, bytes_accessed=nbytes, transcendentals=exps)


CUT_ROWS = 256


def cut_pairs(w_ref, out_ref, half, values):
    cols = pl.ds(pl.multiple_of(values * HD + half * HALF, HALF), HALF)
    pairs = []
    for r in range(0, QUARTER, CUT_ROWS):
        rows = slice(r, r + CUT_ROWS)
        pairs.append((w_ref.at[rows, cols], out_ref.at[rows]))
    return pairs


CUT_COPIES = QUARTER // CUT_ROWS


def sort_kernel(tokens_ref, q_ref, w_ref, far_ref, sib_ref, keys_out, values_out, sems):
    core, y_lo = position()
    home, away = half_of(y_lo, WIDE), half_of(1 - y_lo, WIDE)
    half = TOK // 2
    run_copies(
        [
            (tokens_ref.at[:half, away], far_ref.at[:half]),
            (tokens_ref.at[half:, away], far_ref.at[half:]),
            (tokens_ref.at[:half, home], sib_ref.at[:half]),
            (tokens_ref.at[half:, home], sib_ref.at[half:TOK]),
            (q_ref, sib_ref.at[TOK:]),
        ]
        + cut_pairs(w_ref, keys_out, 1 - core, 0)
        + cut_pairs(w_ref, values_out, 1 - core, 1),
        sems,
    )


def sort_inputs(tokens, q, w):
    shapes = [(TOK, WIDE), (TOK + Q_ROWS, WIDE), (QUARTER, HALF), (QUARTER, HALF)]
    return pl.pallas_call(
        sort_kernel,
        in_specs=[HBM] * 3,
        out_specs=[VMEM] * 4,
        out_shape=[pltpu.VMEM(shape, BF) for shape in shapes],
        scratch_shapes=[pltpu.SemaphoreType.DMA((5 + 2 * CUT_COPIES,))],
        compiler_params=PARAMS,
        cost_estimate=cost(0, 12 << 20),
    )(far_away(tokens), far_away(q), far_away(w))


def join_kernel(far_ref, own_ref, sib_ref, after_ref, out_ref, q_ref, sems):
    del after_ref
    core, _ = position()
    cols = half_of(core, HALF)
    run_copies(
        [
            (far_ref, out_ref),
            (own_ref.at[TOK:, cols], q_ref.at[:Q_ROWS]),
            (sib_ref.at[TOK:, cols], q_ref.at[Q_ROWS:]),
        ],
        sems,
    )


def join(far, own, sib, after):
    return pl.pallas_call(
        join_kernel,
        in_specs=[ANY] * 4,
        out_specs=[VMEM] * 2,
        out_shape=[pltpu.VMEM((TOK, WIDE), BF), pltpu.VMEM((2 * Q_ROWS, HALF), BF)],
        scratch_shapes=[pltpu.SemaphoreType.DMA((3,))],
        compiler_params=PARAMS,
        cost_estimate=cost(0, 1 << 20),
    )(far, own, sib, after)


def cut_kernel(w_ref, after_ref, keys_out, values_out, sems):
    del after_ref
    core, _ = position()
    run_copies(cut_pairs(w_ref, keys_out, core, 0) + cut_pairs(w_ref, values_out, core, 1), sems)


def cut_weights(w, after):
    return pl.pallas_call(
        cut_kernel,
        in_specs=[HBM, ANY],
        out_specs=[VMEM] * 2,
        out_shape=[pltpu.VMEM((QUARTER, HALF), BF) for _ in range(2)],
        scratch_shapes=[pltpu.SemaphoreType.DMA((2 * CUT_COPIES,))],
        compiler_params=PARAMS,
        cost_estimate=cost(0, 8 << 20),
    )(far_away(w), after)


def project_kernel(*refs, rows, extra, parts):
    n, m = len(rows), len(parts)
    pieces, own_refs, sib_refs = refs[:n], refs[n : n + m], refs[n + m : n + 2 * m]
    outs, x_ref, sems = refs[n + 2 * m + extra : -2], refs[-2], refs[-1]
    core, _ = position()
    pairs, start = [], 0
    for piece, count in zip(pieces, rows):
        pairs.append((piece.at[:count], x_ref.at[start : start + count]))
        start += count
    run_copies(pairs, sems)
    half = start // 2
    x_own, x_other = x_ref[:, half_of(core, QUARTER)], x_ref[:, half_of(1 - core, QUARTER)]
    for i in range(m):
        total = jnp.dot(x_other, sib_refs[i][...], preferred_element_type=F32)
        total += jnp.dot(x_own, own_refs[i][...], preferred_element_type=F32)
        for k, out in enumerate(outs):
            out[:, i * HALF : (i + 1) * HALF] = total[k * half : (k + 1) * half].astype(out.dtype)


def project(pieces, own_w, sib_w, parts, dtype, after=()):
    rows = [TOK] * len(pieces)
    total = sum(rows)
    wide = len(parts) * HALF
    args = list(pieces) + [own_w[i] for i in parts] + [sib_w[i] for i in parts] + list(after)
    return pl.pallas_call(
        functools.partial(project_kernel, rows=rows, extra=len(after), parts=parts),
        in_specs=[ANY] * len(pieces) + [VMEM] * (2 * len(parts)) + [ANY] * len(after),
        out_specs=[VMEM] * 2,
        out_shape=[pltpu.VMEM((total // 2, wide), dtype) for _ in range(2)],
        scratch_shapes=[pltpu.VMEM((total, WIDE), BF), pltpu.SemaphoreType.DMA((len(pieces),))],
        compiler_params=pltpu.CompilerParams(vmem_limit_bytes=14 << 20),
        cost_estimate=cost(2 * total * WIDE * wide, 4 * WIDE * wide),
    )(*args)


def softmax_of(q, k):
    scores = lax.dot_general(q, k, (((1,), (1,)), ((), ())), preferred_element_type=F32) * (1.0 / math.sqrt(HS))
    scores = jnp.exp(scores - jnp.max(scores, axis=1, keepdims=True))
    return (scores / jnp.sum(scores, axis=1, keepdims=True)).astype(BF)


def weigh_kernel(near0, near1, far0, far1, own_ref, sib_ref, q_far, out_ref):
    core, _ = position()
    for head in range(HEADS // 2):
        cols = slice(head * HS, (head + 1) * HS)
        global_cols = pl.ds(pl.multiple_of(core * HALF + head * HS, HS), HS)
        q = jnp.concatenate([own_ref[TOK:, global_cols], sib_ref[TOK:, global_cols], q_far[:, cols]], axis=0)
        for batch, (near, far) in enumerate(((near0, far0), (near1, far1))):
            k = near[:, cols] + far[:, cols].astype(F32)
            out_ref[batch * (HEADS // 2) + head] = softmax_of(q, k.astype(BF))


def weigh(near, far, queries):
    args = [*near, *far, *queries]
    return pl.pallas_call(
        weigh_kernel,
        in_specs=[VMEM] * len(args),
        out_specs=VMEM,
        out_shape=pltpu.VMEM((HEADS, S, TOK), BF),
        compiler_params=PARAMS,
        cost_estimate=cost(2 * HEADS * S * TOK * HS, 4 << 20, HEADS * S * TOK),
    )(*args)


def update_kernel(weights_ref, near0, near1, far0, far1, gate_ref, out_ref):
    core, y_lo = position()
    place = y_lo * 2 + core
    for head in range(HEADS // 2):
        cols = slice(head * HS, (head + 1) * HS)
        near_cols = slice(HALF + head * HS, HALF + (head + 1) * HS)
        gate = gate_ref[:, pl.ds(pl.multiple_of(core * HALF + head * HS, HS), HS)]
        terms = []
        for _ in range(3):
            terms.append(gate.astype(BF))
            gate = gate - terms[-1].astype(F32)
        gate = jnp.concatenate([t.astype(F32) for t in terms] + [jnp.zeros((GATE_ROWS - 3, HS), F32)], axis=0).astype(BF)
        for batch, (near, far) in enumerate(((near0, far0), (near1, far1))):
            v = near[:, near_cols] + far[:, cols].astype(F32)
            first = batch * (HEADS // 2) + head
            update = jnp.dot(weights_ref[first], v.astype(BF), preferred_element_type=F32).astype(BF)
            for i in range(S // BLOCK):
                at = first * (S // BLOCK) + (place ^ i)
                out_ref[at, :BLOCK] = update[i * BLOCK : (i + 1) * BLOCK]
                out_ref[at, BLOCK:] = gate


def updates(weights, near, far, gate):
    args = [weights, *near, *far, gate]
    return pl.pallas_call(
        update_kernel,
        in_specs=[VMEM] * len(args),
        out_specs=VMEM,
        out_shape=pltpu.VMEM((SEG, BLOCK + GATE_ROWS, HS), BF),
        compiler_params=PARAMS,
        cost_estimate=cost(2 * HEADS * S * TOK * HS, 4 << 20),
    )(*args)


def scan_kernel(update_ref, out_ref):
    def step(i, carry):
        terms = update_ref[i, BLOCK:].astype(F32)
        gate = terms[0:1] + terms[1:2] + terms[2:3]
        carry = gate * carry + update_ref[i, :BLOCK].astype(F32)
        out_ref[i] = carry.astype(BF)
        return carry

    lax.fori_loop(0, SEG, step, jnp.zeros((BLOCK, HS), F32), unroll=8)


def scan(update):
    return pl.pallas_call(
        scan_kernel,
        in_specs=[VMEM],
        out_specs=VMEM,
        out_shape=pltpu.VMEM((SEG, BLOCK, HS), BF),
        compiler_params=PARAMS,
        cost_estimate=cost(2 * SEG * BLOCK * HS, 4 * SEG * BLOCK * HS),
    )(here(update))


def place_kernel(own_ref, other_ref, out_ref, sems):
    core, _ = position()
    pairs = []
    for batch, (ref, half) in enumerate(((own_ref, core), (other_ref, 1 - core))):
        for j in range(HEADS // 2):
            cols = pl.ds(pl.multiple_of(half * HALF + j * HS, HS), HS)
            pairs.append((ref.at[batch, j], out_ref.at[:, cols]))
    run_copies(pairs, sems)


def place(own, other):
    return pl.pallas_call(
        place_kernel,
        in_specs=[VMEM, VMEM],
        out_specs=ANY,
        out_shape=jax.ShapeDtypeStruct((S, HD), BF),
        scratch_shapes=[pltpu.SemaphoreType.DMA((HEADS,))],
        compiler_params=PARAMS,
        cost_estimate=cost(0, 4 * S * HD),
    )(here(own), here(other))


def spread(value):
    return lax.all_to_all(value, "seg", 0, 0, tiled=True)


def body(tokens, w_kv, q_state, decay):
    to_far, to_sib, to_sib_k, to_sib_v = sort_inputs(tokens[0], q_state, w_kv)
    sib_w = send(to_sib_k, SIB), send(to_sib_v, SIB)
    sib = send(to_sib, SIB)
    own_w = cut_weights(w_kv, to_sib)
    met, queries = join(send(to_far, OUT), to_sib, sib, own_w[0])
    away = [met, send(met, SIB)]
    queries = send(queries, OUT)

    first, second = project(away, own_w, sib_w, (0,), BF)
    far_k = send(first, BACK), send(second, OUT)
    first, second = project(away, own_w, sib_w, (1,), BF, (first,))
    far_v = send(first, BACK), send(second, OUT)
    near = project([to_sib, sib], own_w, sib_w, (0, 1), F32, (queries,))
    weights = weigh(near, far_k, (to_sib, sib, queries))
    states = spread(scan(spread(updates(weights, near, far_v, decay))))
    other = send(states, SIB)
    shape = (2, HEADS // 2, S, HS)
    return place(states.reshape(shape), other.reshape(shape))[None, None]


def solution(mesh):
    return jax.shard_map(
        body,
        mesh=mesh,
        in_specs=(P("fsdp", "seg", None), P("fsdp", None), P("fsdp", None), P("seg", None)),
        out_specs=P("fsdp", "seg", None, None),
        check_vma=False,
    )
```

```python
import functools
import math

import jax
import jax.numpy as jnp
from jax import lax
from jax.experimental import pallas as pl
from jax.experimental.pallas import tpu as pltpu
from jax.sharding import PartitionSpec as P

HEADS = 16
HS = 128
S = 256
SEG = 64
TOK = 128
D = 4096
HD = 2048
QUARTER = D // 4
HALF = HD // 2
BOTH = ("seg", "fsdp")
BF = jnp.bfloat16
F32 = jnp.float32


def flat(y, x, z, core):
    return (((y // 2) * 4 + x) * 8 + z) * 4 + (y % 2) * 2 + core


def moves(steps, dc=0):
    pairs = []
    for y in range(4):
        for x in range(4):
            for z in range(8):
                for core in range(2):
                    pairs.append((flat(y, x, z, core), flat((y + steps[core]) % 4, x, z, (core + dc) % 2)))
    return pairs


OUT, BACK, SIB = moves((1, -1)), moves((-1, 1)), moves((0, 0), 1)


def send(value, pairs):
    return lax.ppermute(value, BOTH, pairs)


TILE = 256
WIDE = 2 * QUARTER
Q_ROWS = S // 4
BLOCK = S // 4
GATE_ROWS = 8

ANY = pl.BlockSpec(memory_space=pl.ANY)
HBM = pl.BlockSpec(memory_space=pltpu.HBM)
VMEM = pl.BlockSpec(memory_space=pltpu.VMEM)


def here(value):
    return pltpu.with_memory_space_constraint(value, pltpu.VMEM)


def far_away(value):
    return pltpu.with_memory_space_constraint(value, pltpu.HBM)


def position():
    fsdp = lax.axis_index("fsdp")
    return fsdp % 2, fsdp // 2


def half_of(which, size):
    return pl.ds(pl.multiple_of(which * size, size), size)


def run_copies(pairs, sems):
    todo = [pltpu.make_async_copy(a, b, sems.at[i]) for i, (a, b) in enumerate(pairs)]
    for c in todo:
        c.start()
    for c in todo:
        c.wait()


PARAMS = pltpu.CompilerParams(vmem_limit_bytes=8 << 20)


def cost(flops, nbytes, exps=0):
    return pl.CostEstimate(flops=flops, bytes_accessed=nbytes, transcendentals=exps)


CUT_ROWS = 256


def cut_pairs(w_ref, out_ref, half, values):
    cols = pl.ds(pl.multiple_of(values * HD + half * HALF, HALF), HALF)
    pairs = []
    for r in range(0, QUARTER, CUT_ROWS):
        rows = slice(r, r + CUT_ROWS)
        pairs.append((w_ref.at[rows, cols], out_ref.at[rows]))
    return pairs


CUT_COPIES = QUARTER // CUT_ROWS


def sort_kernel(tokens_ref, q_ref, w_ref, far_ref, sib_ref, keys_out, values_out, sems):
    core, y_lo = position()
    home, away = half_of(y_lo, WIDE), half_of(1 - y_lo, WIDE)
    half = TOK // 2
    run_copies(
        [
            (tokens_ref.at[:half, away], far_ref.at[:half]),
            (tokens_ref.at[half:, away], far_ref.at[half:]),
            (tokens_ref.at[:half, home], sib_ref.at[:half]),
            (tokens_ref.at[half:, home], sib_ref.at[half:TOK]),
            (q_ref, sib_ref.at[TOK:]),
        ]
        + cut_pairs(w_ref, keys_out, 1 - core, 0)
        + cut_pairs(w_ref, values_out, 1 - core, 1),
        sems,
    )


def sort_inputs(tokens, q, w):
    shapes = [(TOK, WIDE), (TOK + Q_ROWS, WIDE), (QUARTER, HALF), (QUARTER, HALF)]
    return pl.pallas_call(
        sort_kernel,
        in_specs=[HBM] * 3,
        out_specs=[VMEM] * 4,
        out_shape=[pltpu.VMEM(shape, BF) for shape in shapes],
        scratch_shapes=[pltpu.SemaphoreType.DMA((5 + 2 * CUT_COPIES,))],
        compiler_params=PARAMS,
        cost_estimate=cost(0, 12 << 20),
    )(far_away(tokens), far_away(q), far_away(w))


def join_kernel(far_ref, own_ref, sib_ref, after_ref, out_ref, q_ref, sems):
    del after_ref
    core, _ = position()
    cols = half_of(core, HALF)
    run_copies(
        [
            (far_ref, out_ref),
            (own_ref.at[TOK:, cols], q_ref.at[:Q_ROWS]),
            (sib_ref.at[TOK:, cols], q_ref.at[Q_ROWS:]),
        ],
        sems,
    )


def join(far, own, sib, after):
    return pl.pallas_call(
        join_kernel,
        in_specs=[ANY] * 4,
        out_specs=[VMEM] * 2,
        out_shape=[pltpu.VMEM((TOK, WIDE), BF), pltpu.VMEM((2 * Q_ROWS, HALF), BF)],
        scratch_shapes=[pltpu.SemaphoreType.DMA((3,))],
        compiler_params=PARAMS,
        cost_estimate=cost(0, 1 << 20),
    )(far, own, sib, after)


def cut_kernel(w_ref, after_ref, keys_out, values_out, sems):
    del after_ref
    core, _ = position()
    run_copies(cut_pairs(w_ref, keys_out, core, 0) + cut_pairs(w_ref, values_out, core, 1), sems)


def cut_weights(w, after):
    return pl.pallas_call(
        cut_kernel,
        in_specs=[HBM, ANY],
        out_specs=[VMEM] * 2,
        out_shape=[pltpu.VMEM((QUARTER, HALF), BF) for _ in range(2)],
        scratch_shapes=[pltpu.SemaphoreType.DMA((2 * CUT_COPIES,))],
        compiler_params=PARAMS,
        cost_estimate=cost(0, 8 << 20),
    )(far_away(w), after)


def project_kernel(*refs, rows, extra, parts):
    n, m = len(rows), len(parts)
    pieces, own_refs, sib_refs = refs[:n], refs[n : n + m], refs[n + m : n + 2 * m]
    outs, x_ref, sems = refs[n + 2 * m + extra : -2], refs[-2], refs[-1]
    core, _ = position()
    pairs, start = [], 0
    for piece, count in zip(pieces, rows):
        pairs.append((piece.at[:count], x_ref.at[start : start + count]))
        start += count
    run_copies(pairs, sems)
    half = start // 2
    x_own, x_other = x_ref[:, half_of(core, QUARTER)], x_ref[:, half_of(1 - core, QUARTER)]
    for i in range(m):
        total = jnp.dot(x_other, sib_refs[i][...], preferred_element_type=F32)
        total += jnp.dot(x_own, own_refs[i][...], preferred_element_type=F32)
        for k, out in enumerate(outs):
            out[:, i * HALF : (i + 1) * HALF] = total[k * half : (k + 1) * half].astype(out.dtype)


def project(pieces, own_w, sib_w, parts, dtype, after=()):
    rows = [TOK] * len(pieces)
    total = sum(rows)
    wide = len(parts) * HALF
    args = list(pieces) + [own_w[i] for i in parts] + [sib_w[i] for i in parts] + list(after)
    return pl.pallas_call(
        functools.partial(project_kernel, rows=rows, extra=len(after), parts=parts),
        in_specs=[ANY] * len(pieces) + [VMEM] * (2 * len(parts)) + [ANY] * len(after),
        out_specs=[VMEM] * 2,
        out_shape=[pltpu.VMEM((total // 2, wide), dtype) for _ in range(2)],
        scratch_shapes=[pltpu.VMEM((total, WIDE), BF), pltpu.SemaphoreType.DMA((len(pieces),))],
        compiler_params=pltpu.CompilerParams(vmem_limit_bytes=14 << 20),
        cost_estimate=cost(2 * total * WIDE * wide, 4 * WIDE * wide),
    )(*args)


def softmax_of(q, k):
    scores = lax.dot_general(q, k, (((1,), (1,)), ((), ())), preferred_element_type=F32) * (1.0 / math.sqrt(HS))
    scores = jnp.exp(scores - jnp.max(scores, axis=1, keepdims=True))
    return (scores / jnp.sum(scores, axis=1, keepdims=True)).astype(BF)


def weigh_kernel(near0, near1, far0, far1, own_ref, sib_ref, q_far, out_ref):
    core, _ = position()
    for head in range(HEADS // 2):
        cols = slice(head * HS, (head + 1) * HS)
        global_cols = pl.ds(pl.multiple_of(core * HALF + head * HS, HS), HS)
        q = jnp.concatenate([own_ref[TOK:, global_cols], sib_ref[TOK:, global_cols], q_far[:, cols]], axis=0)
        for batch, (near, far) in enumerate(((near0, far0), (near1, far1))):
            k = near[:, cols] + far[:, cols].astype(F32)
            out_ref[batch * (HEADS // 2) + head] = softmax_of(q, k.astype(BF))


def weigh(near, far, queries):
    args = [*near, *far, *queries]
    return pl.pallas_call(
        weigh_kernel,
        in_specs=[VMEM] * len(args),
        out_specs=VMEM,
        out_shape=pltpu.VMEM((HEADS, S, TOK), BF),
        compiler_params=PARAMS,
        cost_estimate=cost(2 * HEADS * S * TOK * HS, 4 << 20, HEADS * S * TOK),
    )(*args)


def update_kernel(weights_ref, near0, near1, far0, far1, gate_ref, out_ref):
    core, y_lo = position()
    place = y_lo * 2 + core
    for head in range(HEADS // 2):
        cols = slice(head * HS, (head + 1) * HS)
        near_cols = slice(HALF + head * HS, HALF + (head + 1) * HS)
        gate = gate_ref[:, pl.ds(pl.multiple_of(core * HALF + head * HS, HS), HS)]
        terms = []
        for _ in range(3):
            terms.append(gate.astype(BF))
            gate = gate - terms[-1].astype(F32)
        gate = jnp.concatenate([t.astype(F32) for t in terms] + [jnp.zeros((GATE_ROWS - 3, HS), F32)], axis=0).astype(BF)
        for batch, (near, far) in enumerate(((near0, far0), (near1, far1))):
            v = near[:, near_cols] + far[:, cols].astype(F32)
            first = batch * (HEADS // 2) + head
            update = jnp.dot(weights_ref[first], v.astype(BF), preferred_element_type=F32).astype(BF)
            for i in range(S // BLOCK):
                at = first * (S // BLOCK) + (place ^ i)
                out_ref[at, :BLOCK] = update[i * BLOCK : (i + 1) * BLOCK]
                out_ref[at, BLOCK:] = gate


def updates(weights, near, far, gate):
    args = [weights, *near, *far, gate]
    return pl.pallas_call(
        update_kernel,
        in_specs=[VMEM] * len(args),
        out_specs=VMEM,
        out_shape=pltpu.VMEM((SEG, BLOCK + GATE_ROWS, HS), BF),
        compiler_params=PARAMS,
        cost_estimate=cost(2 * HEADS * S * TOK * HS, 4 << 20),
    )(*args)


ORDER = [seg for z in range(8) for seg in range(z, SEG, 8)]


def scan_kernel(update_ref, out_ref):
    carry = jnp.zeros((BLOCK, HS), F32)
    for seg in range(SEG):
        i = ORDER.index(seg)
        terms = update_ref[i, BLOCK:].astype(F32)
        gate = terms[0:1] + terms[1:2] + terms[2:3]
        carry = gate * carry + update_ref[i, :BLOCK].astype(F32)
        out_ref[i] = carry.astype(BF)


def scan(update):
    return pl.pallas_call(
        scan_kernel,
        in_specs=[VMEM],
        out_specs=VMEM,
        out_shape=pltpu.VMEM((SEG, BLOCK, HS), BF),
        compiler_params=PARAMS,
        cost_estimate=cost(2 * SEG * BLOCK * HS, 4 * SEG * BLOCK * HS),
    )(here(update))


def half_kernel(states_ref, out_ref, sems):
    run_copies([(states_ref.at[HEADS // 2 * (S // BLOCK) :], out_ref)], sems)


def other_half(states):
    return pl.pallas_call(
        half_kernel,
        in_specs=[ANY],
        out_specs=VMEM,
        out_shape=pltpu.VMEM((SEG // 2, BLOCK, HS), BF),
        scratch_shapes=[pltpu.SemaphoreType.DMA((1,))],
        compiler_params=PARAMS,
        cost_estimate=cost(0, 1 << 20),
    )(states)


def place_kernel(states_ref, *refs, own):
    out_ref, sems = refs[-2:]
    core, _ = position()
    half = core if own else 1 - core
    pairs = []
    for j in range(HEADS // 2):
        cols = pl.ds(pl.multiple_of(half * HALF + j * HS, HS), HS)
        pairs.append((states_ref.at[j], out_ref.at[:, cols]))
    run_copies(pairs, sems)


def place(states, out):
    first = out is None
    return pl.pallas_call(
        functools.partial(place_kernel, own=first),
        in_specs=[VMEM] if first else [VMEM, ANY],
        out_specs=ANY,
        out_shape=jax.ShapeDtypeStruct((S, HD), BF),
        input_output_aliases={} if first else {1: 0},
        scratch_shapes=[pltpu.SemaphoreType.DMA((HEADS // 2,))],
        compiler_params=PARAMS,
        cost_estimate=cost(0, 2 * S * HD),
    )(*([states] if first else [states, out]))


def spread(value):
    return lax.all_to_all(value, "seg", 0, 0, tiled=True, axis_index_groups=[ORDER])


def body(tokens, w_kv, q_state, decay):
    to_far, to_sib, to_sib_k, to_sib_v = sort_inputs(tokens[0], q_state, w_kv)
    sib_w = send(to_sib_k, SIB), send(to_sib_v, SIB)
    sib = send(to_sib, SIB)
    own_w = cut_weights(w_kv, to_sib)
    met, queries = join(send(to_far, OUT), to_sib, sib, own_w[0])
    away = [met, send(met, SIB)]
    queries = send(queries, OUT)

    first, second = project(away, own_w, sib_w, (0,), BF)
    far_k = send(first, BACK), send(second, OUT)
    first, second = project(away, own_w, sib_w, (1,), BF, (first,))
    far_v = send(first, BACK), send(second, OUT)
    near = project([to_sib, sib], own_w, sib_w, (0, 1), F32, (queries,))
    weights = weigh(near, far_k, (to_sib, sib, queries))
    states = spread(scan(spread(updates(weights, near, far_v, decay))))
    other = send(other_half(states), SIB)
    out = place(states.reshape(HEADS, S, HS), None)
    return place(other.reshape(HEADS // 2, S, HS), out)[None, None]


def solution(mesh):
    return jax.shard_map(
        body,
        mesh=mesh,
        in_specs=(P("fsdp", "seg", None), P("fsdp", None), P("fsdp", None), P("seg", None)),
        out_specs=P("fsdp", "seg", None, None),
        check_vma=False,
    )
```

```python
import functools
import math

import jax
import jax.numpy as jnp
from jax import lax
from jax.experimental import pallas as pl
from jax.experimental.pallas import tpu as pltpu
from jax.sharding import PartitionSpec as P

HEADS = 16
HS = 128
S = 256
SEG = 64
TOK = 128
D = 4096
HD = 2048
QUARTER = D // 4
HALF = HD // 2
BOTH = ("seg", "fsdp")
BF = jnp.bfloat16
F32 = jnp.float32


def flat(y, x, z, core):
    return (((y // 2) * 4 + x) * 8 + z) * 4 + (y % 2) * 2 + core


def moves(steps, dc=0):
    pairs = []
    for y in range(4):
        for x in range(4):
            for z in range(8):
                for core in range(2):
                    pairs.append((flat(y, x, z, core), flat((y + steps[core]) % 4, x, z, (core + dc) % 2)))
    return pairs


OUT, BACK, SIB = moves((1, -1)), moves((-1, 1)), moves((0, 0), 1)


def send(value, pairs):
    return lax.ppermute(value, BOTH, pairs)


TILE = 256
WIDE = 2 * QUARTER
Q_ROWS = S // 4
BLOCK = S // 4
GATE_ROWS = 8

ANY = pl.BlockSpec(memory_space=pl.ANY)
HBM = pl.BlockSpec(memory_space=pltpu.HBM)
VMEM = pl.BlockSpec(memory_space=pltpu.VMEM)


def here(value):
    return pltpu.with_memory_space_constraint(value, pltpu.VMEM)


def far_away(value):
    return pltpu.with_memory_space_constraint(value, pltpu.HBM)


def position():
    fsdp = lax.axis_index("fsdp")
    return fsdp % 2, fsdp // 2


def half_of(which, size):
    return pl.ds(pl.multiple_of(which * size, size), size)


def run_copies(pairs, sems):
    todo = [pltpu.make_async_copy(a, b, sems.at[i]) for i, (a, b) in enumerate(pairs)]
    for c in todo:
        c.start()
    for c in todo:
        c.wait()


PARAMS = pltpu.CompilerParams(vmem_limit_bytes=8 << 20)


def cost(flops, nbytes, exps=0):
    return pl.CostEstimate(flops=flops, bytes_accessed=nbytes, transcendentals=exps)


CUT_ROWS = 256


def cut_pairs(w_ref, out_ref, half, values):
    cols = pl.ds(pl.multiple_of(values * HD + half * HALF, HALF), HALF)
    pairs = []
    for r in range(0, QUARTER, CUT_ROWS):
        rows = slice(r, r + CUT_ROWS)
        pairs.append((w_ref.at[rows, cols], out_ref.at[rows]))
    return pairs


CUT_COPIES = QUARTER // CUT_ROWS


def sort_kernel(tokens_ref, q_ref, w_ref, far_ref, sib_ref, keys_out, values_out, sems):
    core, y_lo = position()
    home, away = half_of(y_lo, WIDE), half_of(1 - y_lo, WIDE)
    half = TOK // 2
    run_copies(
        [
            (tokens_ref.at[:half, away], far_ref.at[:half]),
            (tokens_ref.at[half:, away], far_ref.at[half:]),
            (tokens_ref.at[:half, home], sib_ref.at[:half]),
            (tokens_ref.at[half:, home], sib_ref.at[half:TOK]),
            (q_ref, sib_ref.at[TOK:]),
        ]
        + cut_pairs(w_ref, keys_out, 1 - core, 0)
        + cut_pairs(w_ref, values_out, 1 - core, 1),
        sems,
    )


def sort_inputs(tokens, q, w):
    shapes = [(TOK, WIDE), (TOK + Q_ROWS, WIDE), (QUARTER, HALF), (QUARTER, HALF)]
    return pl.pallas_call(
        sort_kernel,
        in_specs=[HBM] * 3,
        out_specs=[VMEM] * 4,
        out_shape=[pltpu.VMEM(shape, BF) for shape in shapes],
        scratch_shapes=[pltpu.SemaphoreType.DMA((5 + 2 * CUT_COPIES,))],
        compiler_params=PARAMS,
        cost_estimate=cost(0, 12 << 20),
    )(far_away(tokens), far_away(q), far_away(w))


def join_kernel(far_ref, own_ref, sib_ref, after_ref, out_ref, q_ref, sems):
    del after_ref
    core, _ = position()
    cols = half_of(core, HALF)
    run_copies(
        [
            (far_ref, out_ref),
            (own_ref.at[TOK:, cols], q_ref.at[:Q_ROWS]),
            (sib_ref.at[TOK:, cols], q_ref.at[Q_ROWS:]),
        ],
        sems,
    )


def join(far, own, sib, after):
    return pl.pallas_call(
        join_kernel,
        in_specs=[ANY] * 4,
        out_specs=[VMEM] * 2,
        out_shape=[pltpu.VMEM((TOK, WIDE), BF), pltpu.VMEM((2 * Q_ROWS, HALF), BF)],
        scratch_shapes=[pltpu.SemaphoreType.DMA((3,))],
        compiler_params=PARAMS,
        cost_estimate=cost(0, 1 << 20),
    )(far, own, sib, after)


def cut_kernel(w_ref, after_ref, keys_out, values_out, sems):
    del after_ref
    core, _ = position()
    run_copies(cut_pairs(w_ref, keys_out, core, 0) + cut_pairs(w_ref, values_out, core, 1), sems)


def cut_weights(w, after):
    return pl.pallas_call(
        cut_kernel,
        in_specs=[HBM, ANY],
        out_specs=[VMEM] * 2,
        out_shape=[pltpu.VMEM((QUARTER, HALF), BF) for _ in range(2)],
        scratch_shapes=[pltpu.SemaphoreType.DMA((2 * CUT_COPIES,))],
        compiler_params=PARAMS,
        cost_estimate=cost(0, 8 << 20),
    )(far_away(w), after)


def project_kernel(*refs, rows, extra, parts):
    n, m = len(rows), len(parts)
    pieces, own_refs, sib_refs = refs[:n], refs[n : n + m], refs[n + m : n + 2 * m]
    outs, x_ref, sems = refs[n + 2 * m + extra : -2], refs[-2], refs[-1]
    core, _ = position()
    pairs, start = [], 0
    for piece, count in zip(pieces, rows):
        pairs.append((piece.at[:count], x_ref.at[start : start + count]))
        start += count
    run_copies(pairs, sems)
    x_own, x_other = x_ref[:, half_of(core, QUARTER)], x_ref[:, half_of(1 - core, QUARTER)]
    for i in range(m):
        total = jnp.dot(x_other, sib_refs[i][...], preferred_element_type=F32)
        total += jnp.dot(x_own, own_refs[i][...], preferred_element_type=F32)
        for k, out in enumerate(outs):
            out[:, i * HALF : (i + 1) * HALF] = total[k * TOK : (k + 1) * TOK].astype(out.dtype)


def project(pieces, own_w, sib_w, parts, dtype, after=()):
    rows = [TOK] * len(pieces)
    total = sum(rows)
    wide = len(parts) * HALF
    args = list(pieces) + [own_w[i] for i in parts] + [sib_w[i] for i in parts] + list(after)
    return pl.pallas_call(
        functools.partial(project_kernel, rows=rows, extra=len(after), parts=parts),
        in_specs=[ANY] * len(pieces) + [VMEM] * (2 * len(parts)) + [ANY] * len(after),
        out_specs=[VMEM] * len(pieces),
        out_shape=[pltpu.VMEM((TOK, wide), dtype) for _ in pieces],
        scratch_shapes=[pltpu.VMEM((total, WIDE), BF), pltpu.SemaphoreType.DMA((len(pieces),))],
        compiler_params=pltpu.CompilerParams(vmem_limit_bytes=14 << 20),
        cost_estimate=cost(2 * total * WIDE * wide, 4 * WIDE * wide),
    )(*args)


def softmax_of(q, k):
    scores = lax.dot_general(q, k, (((1,), (1,)), ((), ())), preferred_element_type=F32) * (1.0 / math.sqrt(HS))
    scores = jnp.exp(scores - jnp.max(scores, axis=1, keepdims=True))
    return (scores / jnp.sum(scores, axis=1, keepdims=True)).astype(BF)


def weigh_kernel(near0, near1, far0, far1, own_ref, sib_ref, q_far, out_ref):
    core, _ = position()
    for head in range(HEADS // 2):
        cols = slice(head * HS, (head + 1) * HS)
        global_cols = pl.ds(pl.multiple_of(core * HALF + head * HS, HS), HS)
        q = jnp.concatenate([own_ref[TOK:, global_cols], sib_ref[TOK:, global_cols], q_far[:, cols]], axis=0)
        for batch, (near, far) in enumerate(((near0, far0), (near1, far1))):
            k = near[:, cols] + far[:, cols].astype(F32)
            out_ref[batch * (HEADS // 2) + head] = softmax_of(q, k.astype(BF))


def weigh(near, far, queries):
    args = [*near, *far, *queries]
    return pl.pallas_call(
        weigh_kernel,
        in_specs=[VMEM] * len(args),
        out_specs=VMEM,
        out_shape=pltpu.VMEM((HEADS, S, TOK), BF),
        compiler_params=PARAMS,
        cost_estimate=cost(2 * HEADS * S * TOK * HS, 4 << 20, HEADS * S * TOK),
    )(*args)


def update_kernel(weights_ref, near0, near1, far0, far1, gate_ref, out_ref):
    core, y_lo = position()
    place = y_lo * 2 + core
    for head in range(HEADS // 2):
        cols = slice(head * HS, (head + 1) * HS)
        near_cols = slice(HALF + head * HS, HALF + (head + 1) * HS)
        gate = gate_ref[:, pl.ds(pl.multiple_of(core * HALF + head * HS, HS), HS)]
        terms = []
        for _ in range(3):
            terms.append(gate.astype(BF))
            gate = gate - terms[-1].astype(F32)
        gate = jnp.concatenate([t.astype(F32) for t in terms] + [jnp.zeros((GATE_ROWS - 3, HS), F32)], axis=0).astype(BF)
        for batch, (near, far) in enumerate(((near0, far0), (near1, far1))):
            v = near[:, near_cols] + far[:, cols].astype(F32)
            first = batch * (HEADS // 2) + head
            update = jnp.dot(weights_ref[first], v.astype(BF), preferred_element_type=F32).astype(BF)
            for i in range(S // BLOCK):
                at = first * (S // BLOCK) + (place ^ i)
                out_ref[at, :BLOCK] = update[i * BLOCK : (i + 1) * BLOCK]
                out_ref[at, BLOCK:] = gate


def updates(weights, near, far, gate):
    args = [weights, *near, *far, gate]
    return pl.pallas_call(
        update_kernel,
        in_specs=[VMEM] * len(args),
        out_specs=VMEM,
        out_shape=pltpu.VMEM((SEG, BLOCK + GATE_ROWS, HS), BF),
        compiler_params=PARAMS,
        cost_estimate=cost(2 * HEADS * S * TOK * HS, 4 << 20),
    )(*args)


ORDER = [seg for z in range(8) for seg in range(z, SEG, 8)]


def scan_kernel(update_ref, out_ref):
    carry = jnp.zeros((BLOCK, HS), F32)
    for seg in range(SEG):
        i = ORDER.index(seg)
        terms = update_ref[i, BLOCK:].astype(F32)
        gate = terms[0:1] + terms[1:2] + terms[2:3]
        carry = gate * carry + update_ref[i, :BLOCK].astype(F32)
        out_ref[i] = carry.astype(BF)


def scan(update):
    return pl.pallas_call(
        scan_kernel,
        in_specs=[VMEM],
        out_specs=VMEM,
        out_shape=pltpu.VMEM((SEG, BLOCK, HS), BF),
        compiler_params=PARAMS,
        cost_estimate=cost(2 * SEG * BLOCK * HS, 4 * SEG * BLOCK * HS),
    )(here(update))


def half_kernel(states_ref, out_ref, sems):
    run_copies([(states_ref.at[HEADS // 2 * (S // BLOCK) :], out_ref)], sems)


def other_half(states):
    return pl.pallas_call(
        half_kernel,
        in_specs=[ANY],
        out_specs=VMEM,
        out_shape=pltpu.VMEM((SEG // 2, BLOCK, HS), BF),
        scratch_shapes=[pltpu.SemaphoreType.DMA((1,))],
        compiler_params=PARAMS,
        cost_estimate=cost(0, 1 << 20),
    )(states)


def place_kernel(states_ref, *refs, own):
    out_ref, sems = refs[-2:]
    core, _ = position()
    half = core if own else 1 - core
    pairs = []
    for j in range(HEADS // 2):
        cols = pl.ds(pl.multiple_of(half * HALF + j * HS, HS), HS)
        pairs.append((states_ref.at[j], out_ref.at[:, cols]))
    run_copies(pairs, sems)


def place(states, out):
    first = out is None
    return pl.pallas_call(
        functools.partial(place_kernel, own=first),
        in_specs=[VMEM] if first else [VMEM, ANY],
        out_specs=ANY,
        out_shape=jax.ShapeDtypeStruct((S, HD), BF),
        input_output_aliases={} if first else {1: 0},
        scratch_shapes=[pltpu.SemaphoreType.DMA((HEADS // 2,))],
        compiler_params=PARAMS,
        cost_estimate=cost(0, 2 * S * HD),
    )(*([states] if first else [states, out]))


def spread(value):
    return lax.all_to_all(value, "seg", 0, 0, tiled=True, axis_index_groups=[ORDER])


def body(tokens, w_kv, q_state, decay):
    to_far, to_sib, to_sib_k, to_sib_v = sort_inputs(tokens[0], q_state, w_kv)
    sib_w = send(to_sib_k, SIB), send(to_sib_v, SIB)
    sib = send(to_sib, SIB)
    own_w = cut_weights(w_kv, to_sib)
    met, queries = join(send(to_far, OUT), to_sib, sib, own_w[0])
    away = [met, send(met, SIB)]
    queries = send(queries, OUT)

    (first,) = project(away[:1], own_w, sib_w, (0,), BF)
    mine = send(first, BACK)
    (second,) = project(away[1:], own_w, sib_w, (0,), BF, (first,))
    far_k = mine, send(second, OUT)
    first, second = project(away, own_w, sib_w, (1,), BF, (second,))
    far_v = send(first, BACK), send(second, OUT)
    near = project([to_sib, sib], own_w, sib_w, (0, 1), F32, (queries,))
    weights = weigh(near, far_k, (to_sib, sib, queries))
    states = spread(scan(spread(updates(weights, near, far_v, decay))))
    other = send(other_half(states), SIB)
    out = place(states.reshape(HEADS, S, HS), None)
    return place(other.reshape(HEADS // 2, S, HS), out)[None, None]


def solution(mesh):
    return jax.shard_map(
        body,
        mesh=mesh,
        in_specs=(P("fsdp", "seg", None), P("fsdp", None), P("fsdp", None), P("seg", None)),
        out_specs=P("fsdp", "seg", None, None),
        check_vma=False,
    )
```

```python
import functools
import math

import jax
import jax.numpy as jnp
from jax import lax
from jax.experimental import pallas as pl
from jax.experimental.pallas import tpu as pltpu
from jax.sharding import PartitionSpec as P

HEADS = 16
HS = 128
S = 256
SEG = 64
TOK = 128
D = 4096
HD = 2048
QUARTER = D // 4
HALF = HD // 2
BOTH = ("seg", "fsdp")
BF = jnp.bfloat16
F32 = jnp.float32


def flat(y, x, z, core):
    return (((y // 2) * 4 + x) * 8 + z) * 4 + (y % 2) * 2 + core


def moves(steps, dc=0):
    pairs = []
    for y in range(4):
        for x in range(4):
            for z in range(8):
                for core in range(2):
                    pairs.append((flat(y, x, z, core), flat((y + steps[core]) % 4, x, z, (core + dc) % 2)))
    return pairs


OUT, BACK, SIB = moves((1, -1)), moves((-1, 1)), moves((0, 0), 1)


def send(value, pairs):
    return lax.ppermute(value, BOTH, pairs)


TILE = 256
WIDE = 2 * QUARTER
Q_ROWS = S // 4
BLOCK = S // 4
GATE_ROWS = 8

ANY = pl.BlockSpec(memory_space=pl.ANY)
HBM = pl.BlockSpec(memory_space=pltpu.HBM)
VMEM = pl.BlockSpec(memory_space=pltpu.VMEM)


def here(value):
    return pltpu.with_memory_space_constraint(value, pltpu.VMEM)


def far_away(value):
    return pltpu.with_memory_space_constraint(value, pltpu.HBM)


def position():
    fsdp = lax.axis_index("fsdp")
    return fsdp % 2, fsdp // 2


def half_of(which, size):
    return pl.ds(pl.multiple_of(which * size, size), size)


def run_copies(pairs, sems):
    todo = [pltpu.make_async_copy(a, b, sems.at[i]) for i, (a, b) in enumerate(pairs)]
    for c in todo:
        c.start()
    for c in todo:
        c.wait()


PARAMS = pltpu.CompilerParams(vmem_limit_bytes=8 << 20)


def cost(flops, nbytes, exps=0):
    return pl.CostEstimate(flops=flops, bytes_accessed=nbytes, transcendentals=exps)


CUT_ROWS = 256


def cut_pairs(w_ref, out_ref, half, values):
    cols = pl.ds(pl.multiple_of(values * HD + half * HALF, HALF), HALF)
    pairs = []
    for r in range(0, QUARTER, CUT_ROWS):
        rows = slice(r, r + CUT_ROWS)
        pairs.append((w_ref.at[rows, cols], out_ref.at[rows]))
    return pairs


CUT_COPIES = QUARTER // CUT_ROWS


def sort_kernel(tokens_ref, q_ref, w_ref, far_ref, sib_ref, keys_out, values_out, sems):
    core, y_lo = position()
    home, away = half_of(y_lo, WIDE), half_of(1 - y_lo, WIDE)
    half = TOK // 2
    run_copies(
        [
            (tokens_ref.at[:half, away], far_ref.at[:half]),
            (tokens_ref.at[half:, away], far_ref.at[half:]),
            (tokens_ref.at[:half, home], sib_ref.at[:half]),
            (tokens_ref.at[half:, home], sib_ref.at[half:TOK]),
            (q_ref, sib_ref.at[TOK:]),
        ]
        + cut_pairs(w_ref, keys_out, 1 - core, 0)
        + cut_pairs(w_ref, values_out, 1 - core, 1),
        sems,
    )


def sort_inputs(tokens, q, w):
    shapes = [(TOK, WIDE), (TOK + Q_ROWS, WIDE), (QUARTER, HALF), (QUARTER, HALF)]
    return pl.pallas_call(
        sort_kernel,
        in_specs=[HBM] * 3,
        out_specs=[VMEM] * 4,
        out_shape=[pltpu.VMEM(shape, BF) for shape in shapes],
        scratch_shapes=[pltpu.SemaphoreType.DMA((5 + 2 * CUT_COPIES,))],
        compiler_params=PARAMS,
        cost_estimate=cost(0, 12 << 20),
    )(far_away(tokens), far_away(q), far_away(w))


def join_kernel(far_ref, own_ref, sib_ref, after_ref, out_ref, q_ref, sems):
    del after_ref
    core, _ = position()
    cols = half_of(core, HALF)
    run_copies(
        [
            (far_ref, out_ref),
            (own_ref.at[TOK:, cols], q_ref.at[:Q_ROWS]),
            (sib_ref.at[TOK:, cols], q_ref.at[Q_ROWS:]),
        ],
        sems,
    )


def join(far, own, sib, after):
    return pl.pallas_call(
        join_kernel,
        in_specs=[ANY] * 4,
        out_specs=[VMEM] * 2,
        out_shape=[pltpu.VMEM((TOK, WIDE), BF), pltpu.VMEM((2 * Q_ROWS, HALF), BF)],
        scratch_shapes=[pltpu.SemaphoreType.DMA((3,))],
        compiler_params=PARAMS,
        cost_estimate=cost(0, 1 << 20),
    )(far, own, sib, after)


def cut_kernel(w_ref, after_ref, keys_out, values_out, sems):
    del after_ref
    core, _ = position()
    run_copies(cut_pairs(w_ref, keys_out, core, 0) + cut_pairs(w_ref, values_out, core, 1), sems)


def cut_weights(w, after):
    return pl.pallas_call(
        cut_kernel,
        in_specs=[HBM, ANY],
        out_specs=[VMEM] * 2,
        out_shape=[pltpu.VMEM((QUARTER, HALF), BF) for _ in range(2)],
        scratch_shapes=[pltpu.SemaphoreType.DMA((2 * CUT_COPIES,))],
        compiler_params=PARAMS,
        cost_estimate=cost(0, 8 << 20),
    )(far_away(w), after)


def project_kernel(*refs, rows, extra, parts):
    n, m = len(rows), len(parts)
    pieces, own_refs, sib_refs = refs[:n], refs[n : n + m], refs[n + m : n + 2 * m]
    outs, x_ref, sems = refs[n + 2 * m + extra : -2], refs[-2], refs[-1]
    core, _ = position()
    pairs, start = [], 0
    for piece, count in zip(pieces, rows):
        pairs.append((piece.at[:count], x_ref.at[start : start + count]))
        start += count
    run_copies(pairs, sems)
    x_own, x_other = x_ref[:, half_of(core, QUARTER)], x_ref[:, half_of(1 - core, QUARTER)]
    for i in range(m):
        total = jnp.dot(x_other, sib_refs[i][...], preferred_element_type=F32)
        total += jnp.dot(x_own, own_refs[i][...], preferred_element_type=F32)
        for k, out in enumerate(outs):
            out[:, i * HALF : (i + 1) * HALF] = total[k * TOK : (k + 1) * TOK].astype(out.dtype)


def project(pieces, own_w, sib_w, parts, dtype, after=()):
    rows = [TOK] * len(pieces)
    total = sum(rows)
    wide = len(parts) * HALF
    args = list(pieces) + [own_w[i] for i in parts] + [sib_w[i] for i in parts] + list(after)
    return pl.pallas_call(
        functools.partial(project_kernel, rows=rows, extra=len(after), parts=parts),
        in_specs=[ANY] * len(pieces) + [VMEM] * (2 * len(parts)) + [ANY] * len(after),
        out_specs=[VMEM] * len(pieces),
        out_shape=[pltpu.VMEM((TOK, wide), dtype) for _ in pieces],
        scratch_shapes=[pltpu.VMEM((total, WIDE), BF), pltpu.SemaphoreType.DMA((len(pieces),))],
        compiler_params=pltpu.CompilerParams(vmem_limit_bytes=14 << 20),
        cost_estimate=cost(2 * total * WIDE * wide, 4 * WIDE * wide),
    )(*args)


def softmax_of(q, k):
    scores = lax.dot_general(q, k, (((1,), (1,)), ((), ())), preferred_element_type=F32) * (1.0 / math.sqrt(HS))
    scores = jnp.exp(scores - jnp.max(scores, axis=1, keepdims=True))
    return (scores / jnp.sum(scores, axis=1, keepdims=True)).astype(BF)


def weigh_kernel(near0, near1, far0, far1, own_ref, sib_ref, q_far, out_ref):
    core, _ = position()
    for head in range(HEADS // 2):
        cols = slice(head * HS, (head + 1) * HS)
        global_cols = pl.ds(pl.multiple_of(core * HALF + head * HS, HS), HS)
        q = jnp.concatenate([own_ref[TOK:, global_cols], sib_ref[TOK:, global_cols], q_far[:, cols]], axis=0)
        for batch, (near, far) in enumerate(((near0, far0), (near1, far1))):
            k = near[:, cols] + far[:, cols].astype(F32)
            out_ref[batch * (HEADS // 2) + head] = softmax_of(q, k.astype(BF))


def weigh(near, far, queries):
    args = [*near, *far, *queries]
    return pl.pallas_call(
        weigh_kernel,
        in_specs=[VMEM] * len(args),
        out_specs=VMEM,
        out_shape=pltpu.VMEM((HEADS, S, TOK), BF),
        compiler_params=PARAMS,
        cost_estimate=cost(2 * HEADS * S * TOK * HS, 4 << 20, HEADS * S * TOK),
    )(*args)


def update_kernel(weights_ref, near0, near1, far0, far1, gate_ref, out_ref):
    core, y_lo = position()
    place = y_lo * 2 + core
    for head in range(HEADS // 2):
        cols = slice(head * HS, (head + 1) * HS)
        near_cols = slice(HALF + head * HS, HALF + (head + 1) * HS)
        gate = gate_ref[:, pl.ds(pl.multiple_of(core * HALF + head * HS, HS), HS)]
        terms = []
        for _ in range(3):
            terms.append(gate.astype(BF))
            gate = gate - terms[-1].astype(F32)
        gate = jnp.concatenate([t.astype(F32) for t in terms] + [jnp.zeros((GATE_ROWS - 3, HS), F32)], axis=0).astype(BF)
        for batch, (near, far) in enumerate(((near0, far0), (near1, far1))):
            v = near[:, near_cols] + far[:, cols].astype(F32)
            first = batch * (HEADS // 2) + head
            update = jnp.dot(weights_ref[first], v.astype(BF), preferred_element_type=F32).astype(BF)
            for i in range(S // BLOCK):
                at = first * (S // BLOCK) + (place ^ i)
                out_ref[at, :BLOCK] = update[i * BLOCK : (i + 1) * BLOCK]
                out_ref[at, BLOCK:] = gate


def updates(weights, near, far, gate):
    args = [weights, *near, *far, gate]
    return pl.pallas_call(
        update_kernel,
        in_specs=[VMEM] * len(args),
        out_specs=VMEM,
        out_shape=pltpu.VMEM((SEG, BLOCK + GATE_ROWS, HS), BF),
        compiler_params=PARAMS,
        cost_estimate=cost(2 * HEADS * S * TOK * HS, 4 << 20),
    )(*args)


ORDER = [seg for z in range(8) for seg in range(z, SEG, 8)]


def scan_kernel(update_ref, out_ref):
    carry = jnp.zeros((BLOCK, HS), F32)
    for seg in range(SEG):
        i = ORDER.index(seg)
        terms = update_ref[i, BLOCK:].astype(F32)
        gate = terms[0:1] + terms[1:2] + terms[2:3]
        carry = gate * carry + update_ref[i, :BLOCK].astype(F32)
        out_ref[i] = carry.astype(BF)


def scan(update):
    return pl.pallas_call(
        scan_kernel,
        in_specs=[VMEM],
        out_specs=VMEM,
        out_shape=pltpu.VMEM((SEG, BLOCK, HS), BF),
        compiler_params=PARAMS,
        cost_estimate=cost(2 * SEG * BLOCK * HS, 4 * SEG * BLOCK * HS),
    )(here(update))


def half_kernel(states_ref, out_ref, sems):
    run_copies([(states_ref.at[HEADS // 2 * (S // BLOCK) :], out_ref)], sems)


def other_half(states):
    return pl.pallas_call(
        half_kernel,
        in_specs=[ANY],
        out_specs=VMEM,
        out_shape=pltpu.VMEM((SEG // 2, BLOCK, HS), BF),
        scratch_shapes=[pltpu.SemaphoreType.DMA((1,))],
        compiler_params=PARAMS,
        cost_estimate=cost(0, 1 << 20),
    )(states)


def place_kernel(states_ref, *refs, own):
    out_ref, sems = refs[-2:]
    core, _ = position()
    half = core if own else 1 - core
    pairs = []
    for j in range(HEADS // 2):
        cols = pl.ds(pl.multiple_of(half * HALF + j * HS, HS), HS)
        pairs.append((states_ref.at[j], out_ref.at[:, cols]))
    run_copies(pairs, sems)


def place(states, out):
    first = out is None
    return pl.pallas_call(
        functools.partial(place_kernel, own=first),
        in_specs=[VMEM] if first else [VMEM, ANY],
        out_specs=ANY,
        out_shape=jax.ShapeDtypeStruct((S, HD), BF),
        input_output_aliases={} if first else {1: 0},
        scratch_shapes=[pltpu.SemaphoreType.DMA((HEADS // 2,))],
        compiler_params=PARAMS,
        cost_estimate=cost(0, 2 * S * HD),
    )(*([states] if first else [states, out]))


def spread(value):
    return lax.all_to_all(value, "seg", 0, 0, tiled=True, axis_index_groups=[ORDER])


def body(tokens, w_kv, q_state, decay):
    to_far, to_sib, to_sib_k, to_sib_v = sort_inputs(tokens[0], q_state, w_kv)
    sib_w = send(to_sib_k, SIB), send(to_sib_v, SIB)
    sib = send(to_sib, SIB)
    own_w = cut_weights(w_kv, to_sib)
    met, queries = join(send(to_far, OUT), to_sib, sib, own_w[0])
    away = [met, send(met, SIB)]
    queries = send(queries, OUT)

    (first,) = project(away[:1], own_w, sib_w, (0,), BF)
    mine = send(first, BACK)
    (second,) = project(away[1:], own_w, sib_w, (0,), BF, (first,))
    far_k = mine, send(second, OUT)
    (first,) = project(away[:1], own_w, sib_w, (1,), BF, (second,))
    mine = send(first, BACK)
    (second,) = project(away[1:], own_w, sib_w, (1,), BF, (first,))
    far_v = mine, send(second, OUT)
    near = project([to_sib, sib], own_w, sib_w, (0, 1), F32, (queries,))
    weights = weigh(near, far_k, (to_sib, sib, queries))
    states = spread(scan(spread(updates(weights, near, far_v, decay))))
    other = send(other_half(states), SIB)
    out = place(states.reshape(HEADS, S, HS), None)
    return place(other.reshape(HEADS // 2, S, HS), out)[None, None]


def solution(mesh):
    return jax.shard_map(
        body,
        mesh=mesh,
        in_specs=(P("fsdp", "seg", None), P("fsdp", None), P("fsdp", None), P("seg", None)),
        out_specs=P("fsdp", "seg", None, None),
        check_vma=False,
    )
```
